512 devices in a mesh: party: 2 (over core), head: 16 (over z, y_lo), seq: 16 (over y_hi, x).
Axes of the slice: x: 4, y: 8 (y_hi: 4, y_lo: 2; y = y_hi * 2 + y_lo), z: 8, core: 2. Of those that a mesh axis runs over, the one named last changes fastest.
Arguments:
- query_share: bfloat16 [2, 32, 2048, 128], P('party', 'head', 'seq'), may hold values from -6 to 6
- key_share: bfloat16 [2, 32, 2048, 128], P('party', 'head', 'seq'), may hold values from -6 to 6
- value_share: bfloat16 [2, 32, 2048, 128], P('party', 'head', 'seq'), may hold values from -6 to 6
- query_mask: bfloat16 [2, 32, 2048, 128], P('party', 'head', 'seq'), may hold values from -6 to 6
- key_mask: bfloat16 [2, 32, 2048, 128], P('party', 'head', 'seq'), may hold values from -6 to 6
- value_mask: bfloat16 [2, 32, 2048, 128], P('party', 'head', 'seq'), may hold values from -1.5 to 1.5
- score_triple: bfloat16 [2, 32, 2048, 2048], P('party', 'head', 'seq'), may hold values from -6 to 6
- square_triple: bfloat16 [2, 32, 2048, 2048], P('party', 'head', 'seq'), may hold values from -6 to 6
- weight_mask: bfloat16 [2, 32, 2048, 2048], P('party', 'head', 'seq'), may hold values from -0.75 to 0.75
- output_triple: bfloat16 [2, 32, 2048, 128], P('party', 'head', 'seq'), may hold values from -3 to 3
- out_weight: bfloat16 [4096, 2560], P('head'), may hold values from -0.125 to 0.125
Outputs:
- mixed_share: float32 [2, 2048, 2560], P('party', 'seq', 'head')
The draws below stay inside these ranges and needn't reach their ends.
All inputs are finite; a program needn't handle non-finite values.
Results may differ from the reference program's by a relative error of at most 0.0003.
Values may be sent and summed in bfloat16 or wider, within the bound.
A program may use at most 64 MiB of HBM per device.

```python
import jax
import jax.numpy as jnp
from jax import lax

HD = 128
DOUT = 2560
HEADS = 32
SEQ = 2048


def strengthened(entries, key, source, target, shards_of, factor):
    owner, partner = [(jnp.arange(entries.shape[position]) // (entries.shape[position] // shards_of)).reshape([-1 if axis == position else 1 for axis in range(entries.ndim)]) for position in (source, target)]
    chosen = jax.random.permutation(key, shards_of)[partner]
    strong = (owner == chosen) | (owner == (partner + shards_of // 2) % shards_of)
    return jnp.where(strong, factor * entries, entries)


def shard_levels(rng, extent, cuts, least, top_value):
    level, own = 1.0, jax.random.fold_in(rng, 6)
    for dim, parts in cuts:
        steps = jnp.exp(jax.random.uniform(jax.random.fold_in(own, dim), (parts,), jnp.float32, least / len(cuts), top_value / len(cuts)))
        level = level * jnp.repeat(steps, extent[dim] // parts).reshape([-1 if axis == dim else 1 for axis in range(len(extent))])
    return level


def normal_values(own_key, extent, spread, reach, split=(), kind=jnp.bfloat16):
    values = spread * jax.random.normal(own_key, extent, jnp.float32)
    if split:
        values = values * shard_levels(own_key, extent, split, -0.22, 0.18)
    return jnp.clip(values, -reach, reach).astype(kind)


def gaussian_with(stream_key, shape, scale, bound, pieces, heavy, kind=jnp.bfloat16):
    entries = scale * jax.random.normal(stream_key, shape, jnp.float32)
    if pieces:
        entries = entries * shard_levels(stream_key, shape, pieces, -0.22, 0.18)
    return jnp.clip(strengthened(entries, jax.random.fold_in(stream_key, 3), *heavy), -bound, bound).astype(kind)


def setup_inputs(seed: int = 0) -> dict:
    splits = jax.random.split(jax.random.key(seed), 12)
    query_share = normal_values(splits[0], (2, HEADS, SEQ, HD), 1.0, 6.0, ((0, 2), (1, 16), (2, 16)))
    key_share = normal_values(splits[1], (2, HEADS, SEQ, HD), 1.0, 6.0, ((0, 2), (1, 16), (2, 16)))
    value_share = normal_values(splits[2], (2, HEADS, SEQ, HD), 1.0, 6.0, ((0, 2), (1, 16), (2, 16)))
    query_mask = normal_values(splits[3], (2, HEADS, SEQ, HD), 0.5, 6.0, ((0, 2), (1, 16), (2, 16)))
    key_mask = normal_values(splits[4], (2, HEADS, SEQ, HD), 0.5, 6.0, ((0, 2), (1, 16), (2, 16)))
    value_mask = normal_values(splits[5], (2, HEADS, SEQ, HD), 0.1, 1.5, ((0, 2), (1, 16), (2, 16)))
    score_triple = normal_values(splits[6], (2, HEADS, SEQ, SEQ), 0.5, 6.0, ((0, 2), (1, 16), (2, 16)))
    square_triple = normal_values(splits[7], (2, HEADS, SEQ, SEQ), 0.5, 6.0, ((0, 2), (1, 16), (2, 16)))
    weight_mask = normal_values(splits[8], (2, HEADS, SEQ, SEQ), 0.05, 0.75, ((0, 2), (1, 16), (2, 16)))
    output_triple = normal_values(splits[9], (2, HEADS, SEQ, HD), 0.2, 3.0, ((0, 2), (1, 16), (2, 16)))
    out_weight = gaussian_with(splits[10], (HEADS * HD, DOUT), (HEADS * HD) ** -0.5, 0.125, ((0, 16),), (0, 1, 16, 2.0))
    return {"query_share": query_share, "key_share": key_share, "value_share": value_share, "query_mask": query_mask, "key_mask": key_mask, "value_mask": value_mask, "score_triple": score_triple, "square_triple": square_triple, "weight_mask": weight_mask, "output_triple": output_triple, "out_weight": out_weight}


def reference(query_share, key_share, value_share, query_mask, key_mask, value_mask, score_triple, square_triple, weight_mask, output_triple, out_weight):
    highest = lax.Precision.HIGHEST
    leader = jnp.array([1.0, 0.0], dtype=jnp.float32)[:, None, None]
    rows = lax.broadcasted_iota(jnp.int32, (SEQ, SEQ), 0)
    cols = lax.broadcasted_iota(jnp.int32, (SEQ, SEQ), 1)
    visible = cols <= rows
    row_scale = lax.rsqrt((rows + 1).astype(jnp.float32))
    scale_factor = HD ** (-0.5)

    def one_head(index):

        def pick(array):
            return lax.dynamic_index_in_dim(array, index, 1, keepdims=False).astype(jnp.float32)
        query_diff = pick(query_share) - pick(query_mask)
        key_diff = pick(key_share) - pick(key_mask)
        value_diff = pick(value_share) - pick(value_mask)
        opened_query = query_diff[0] + query_diff[1]
        opened_keys = key_diff[0] + key_diff[1]
        opened_values = value_diff[0] + value_diff[1]
        score_part = scale_factor * (jnp.einsum('qd,pkd->pqk', opened_query, pick(key_mask) + leader * opened_keys, precision=highest) + jnp.einsum('pqd,kd->pqk', pick(query_mask), opened_keys, precision=highest))
        opened_scores = score_part[0] + score_part[1]
        triple_here = pick(score_triple)
        share_scores = triple_here + score_part
        square_part = pick(square_triple) + 2.0 * opened_scores * triple_here + leader * opened_scores * opened_scores
        poly = leader * 1.25 + share_scores + 0.25 * square_part
        weights = jnp.where(visible, poly * row_scale, 0.0)
        weight_here = pick(weight_mask)
        weight_diff = weights - weight_here
        opened_weights = weight_diff[0] + weight_diff[1]
        values_all = pick(value_mask) + leader * opened_values
        return pick(output_triple) + jnp.einsum('qk,pkd->pqd', opened_weights, values_all, precision=highest) + jnp.einsum('pqk,kd->pqd', weight_here, opened_values, precision=highest)
    outputs = lax.map(one_head, jnp.arange(HEADS, dtype=jnp.int32))
    weight_all = out_weight.astype(jnp.float32).reshape(HEADS, HD, DOUT)
    return jnp.einsum('hpsd,hdo->pso', outputs, weight_all, precision=highest)
```

```python
import functools

import jax
import jax.numpy as jnp
from jax import lax
from jax.experimental import pallas as pl
from jax.experimental.pallas import tpu as pltpu
from jax.sharding import PartitionSpec as P

F32 = jnp.float32
BF16 = jnp.bfloat16
T = 128
NX, NY, NZ = 4, 4, 8
SLOTS = NX * NY
COLS = 160
CHUNKS = ((0, 3, True, 1), (3, 3, True, -1), (6, 1, False, 1), (7, 1, False, -1))
SUBS = 2
ROWS = COLS // SUBS


def split(value):
    high = value.astype(BF16)
    return high, (value - high.astype(F32)).astype(BF16)


def nt(left, right):
    return lax.dot_general(left, right, (((1,), (1,)), ((), ())), preferred_element_type=F32)


def nn(left, right):
    return lax.dot_general(left, right, (((1,), (0,)), ((), ())), preferred_element_type=F32)


def kernel(
    ks, km, vs, vm, qs, qm, ot, zt, st, wm, ow, out_ref,
    kv, qo, big, wt_in, wt, gat, qa, acc, outs, pt, rsb, fin, fin_rx,
    loc_sem, swp_send, swp_recv, w_sem, g_send, g_recv, h_send, h_recv, r_send, r_recv, y_send, y_recv,
):
    party = lax.axis_index("party")
    head = lax.axis_index("head")
    seq = lax.axis_index("seq")
    z, ylo = head // 2, head % 2
    yh, x = seq // NX, seq % NX
    sib = {"party": 1 - party}

    def at_slot(y, xx):
        return (y % NY) * NX + xx % NX

    def at_z(zz):
        return {"head": (zz % NZ) * 2 + ylo}

    peers = [
        sib,
        {"seq": at_slot(yh, x + 1)},
        {"seq": at_slot(yh, x + NX - 1)},
        {"seq": at_slot(yh + 1, x)},
        {"seq": at_slot(yh + NY - 1, x)},
        at_z(z + 1),
        at_z(z + NZ - 1),
        {"head": z * 2 + 1 - ylo},
    ]
    barrier = pltpu.get_barrier_semaphore()
    for peer in peers:
        pl.semaphore_signal(barrier, inc=1, device_id=peer, device_id_type=pl.DeviceIdType.MESH)

    arrays = [ks, km, vs, vm, qs, qm, ot, zt, st, wm]
    places = [kv.at[i] for i in range(4)] + [qo.at[i] for i in range(3)] + [big.at[i] for i in range(3)]
    locals_ = []
    for i, (src, dst) in enumerate(zip(arrays, places)):
        locals_.append(pltpu.make_async_copy(src.at[0, party], dst.at[party], loc_sem.at[i]))
        locals_[-1].start()
    weights_in = pltpu.make_async_copy(ow, wt_in, w_sem)
    weights_in.start()
    pl.semaphore_wait(barrier, len(peers))
    swaps = []
    for i, (src, dst) in enumerate(zip(arrays, places)):
        swaps.append(
            pltpu.make_async_remote_copy(
                src_ref=src.at[0, 1 - party],
                dst_ref=dst.at[party],
                send_sem=swp_send.at[i],
                recv_sem=swp_recv.at[i],
                device_id=sib,
                device_id_type=pl.DeviceIdType.MESH,
            )
        )
        swaps[-1].start()

    def arrived(i):
        locals_[i].wait()
        swaps[i].wait_recv()

    for i in range(4):
        arrived(i)

    def wide(ref):
        return ref[...].astype(F32)

    kh, kl = split(wide(kv.at[0, 0]) + wide(kv.at[0, 1]))
    bh, bl = split(wide(kv.at[1, 0]) + wide(kv.at[1, 1]))
    dh, dl = split(
        (wide(kv.at[2, 0]) - wide(kv.at[3, 0])) + (wide(kv.at[2, 1]) - wide(kv.at[3, 1]))
    )
    for i, value in enumerate((kh, kl, bh, bl, dh, dl, kv[3, 0], kv[3, 1])):
        gat[seq, i] = value

    sends = []

    def copy(chunk, first, second, y, xx, target):
        start, count = CHUNKS[chunk][:2]
        place = gat.at[at_slot(y, xx), pl.ds(start, count)]
        return pltpu.make_async_remote_copy(
            src_ref=place,
            dst_ref=place,
            send_sem=g_send.at[chunk * 16 + first * 4 + second],
            recv_sem=g_recv.at[chunk * 16 + first * 4 + second],
            device_id={"seq": target},
            device_id_type=pl.DeviceIdType.MESH,
        )

    def send(chunk, first, second, y, xx, along_y, step):
        target = at_slot(yh + step + NY, x) if along_y else at_slot(yh, x + step + NX)
        one = copy(chunk, first, second, y, xx, target)
        one.start()
        sends.append(one)

    def origin(chunk, first, second):
        _, _, y_first, sign = CHUNKS[chunk]
        moves = (0, -sign, sign, 2)
        dy, dx = (moves[first], moves[second]) if y_first else (moves[second], moves[first])
        return yh + dy + NY, x + dx + NX

    def spread_second(chunk, first):
        _, _, y_first, sign = CHUNKS[chunk]
        y, xx = origin(chunk, first, 0)
        send(chunk, first, 1, y, xx, not y_first, sign)
        send(chunk, first, 2, y, xx, not y_first, -sign)

    def receive(chunk, first, second):
        _, _, y_first, sign = CHUNKS[chunk]
        y, xx = origin(chunk, first, second)
        copy(chunk, first, second, y, xx, seq).wait_recv()
        if second == 0:
            if first == 1:
                send(chunk, 3, 0, y, xx, y_first, sign)
            spread_second(chunk, first)
        elif second == 1:
            send(chunk, first, 3, y, xx, not y_first, sign)

    for chunk, (_, _, y_first, sign) in enumerate(CHUNKS):
        send(chunk, 1, 0, yh, x, y_first, sign)
        send(chunk, 2, 0, yh, x, y_first, -sign)
    for chunk in range(4):
        spread_second(chunk, 0)

    for i in range(4, 7):
        arrived(i)
    scale = T ** (-0.5)
    qh, ql = split(scale * (wide(qo.at[0, 0]) + wide(qo.at[0, 1])))
    ah, al = split(-scale * (wide(qo.at[1, 0]) + wide(qo.at[1, 1])))
    for i, value in enumerate((qh, qh, ql, ah, ah, al)):
        qa[:, i * T : (i + 1) * T] = value
    acc[0] = wide(qo.at[2, 0])
    acc[1] = wide(qo.at[2, 1])
    for i in range(7, 10):
        arrived(i)

    def attend(slot):
        cols = pl.ds(pl.multiple_of(slot * T, T), T)
        kh, kl, bh, bl, dh, dl, c0, c1 = [gat[slot, i] for i in range(8)]
        scores = nt(qa[...], jnp.concatenate([kh, kl, kh, bh, bl, bh], axis=1))
        zz = big[0, 0, :, cols].astype(F32) + big[0, 1, :, cols].astype(F32)
        sq = big[1, 0, :, cols].astype(F32) + big[1, 1, :, cols].astype(F32)
        w0 = big[2, 0, :, cols]
        w1 = big[2, 1, :, cols]
        poly = 1.25 + zz + 0.25 * sq + scores * (1.0 + 0.5 * zz + 0.25 * scores)
        row = seq * T + lax.broadcasted_iota(jnp.int32, (T, T), 0)
        col = slot * T + lax.broadcasted_iota(jnp.int32, (T, T), 1)
        weights = jnp.where(col <= row, poly * lax.rsqrt((row + 1).astype(F32)), 0.0)
        lead = weights - w1.astype(F32)
        opened = lead - w0.astype(F32)
        lh, ll = split(lead)
        oh, ol = split(opened)
        both = jnp.concatenate([c0, c1], axis=1)
        mixed = nn(jnp.concatenate([oh, ol], axis=1), jnp.concatenate([both, both], axis=0))
        acc[0] += mixed[:, :T] + nn(
            jnp.concatenate([lh, ll, lh], axis=1), jnp.concatenate([dh, dh, dl], axis=0)
        )
        acc[1] += mixed[:, T:] + nn(
            jnp.concatenate([w1, w1], axis=1), jnp.concatenate([dh, dl], axis=0)
        )

    def attend_at(dy, dx):
        attend(at_slot(yh + dy + NY, x + dx + NX))

    attend_at(0, 0)
    for chunk in range(4):
        receive(chunk, 1, 0)
    for chunk in range(4):
        receive(chunk, 2, 0)
    for chunk in range(4):
        receive(chunk, 0, 1)
    weights_in.wait()

    @pl.loop(0, 20)
    def _(i):
        cols = pl.ds(pl.multiple_of(i * T, T), T)
        wt[cols, :] = wt_in[:, cols].T

    for chunk in range(4):
        receive(chunk, 0, 2)
    for dy, dx in ((1, 0), (-1, 0), (0, 1), (0, -1)):
        attend_at(dy, dx)
    for chunk in range(4):
        receive(chunk, 3, 0)
    for chunk in range(4):
        receive(chunk, 1, 1)
        receive(chunk, 2, 1)
    for chunk in range(4):
        receive(chunk, 0, 3)
        receive(chunk, 1, 2)
        receive(chunk, 2, 2)
        receive(chunk, 3, 1)
    for dy, dx in ((2, 0), (0, 2), (1, 1), (1, -1), (-1, 1), (-1, -1)):
        attend_at(dy, dx)
    for chunk in range(4):
        receive(chunk, 3, 2)
        receive(chunk, 1, 3)
        receive(chunk, 2, 3)
    for dy, dx in ((2, 1), (2, -1), (1, 2), (-1, 2)):
        attend_at(dy, dx)
    for chunk in range(4):
        receive(chunk, 3, 3)
    attend_at(2, 2)

    swap = pltpu.make_async_remote_copy(
        src_ref=acc.at[1 - party],
        dst_ref=outs.at[party],
        send_sem=h_send,
        recv_sem=h_recv,
        device_id=sib,
        device_id_type=pl.DeviceIdType.MESH,
    )
    swap.start()
    outs[party] = acc[party]
    swap.wait_recv()
    oh, ol = split(jnp.concatenate([outs[0], outs[1]], axis=1))
    ohl = jnp.concatenate([oh, ol], axis=1)

    def project(zz):
        rows = pl.ds(pl.multiple_of((zz % NZ) * 2 * COLS, 2 * COLS), 2 * COLS)
        part = wt[rows, :]
        pt[zz % NZ] = nt(jnp.concatenate([part, part], axis=1), ohl)

    ring = []

    def ring_copy(way, step, sub, src):
        index = (way * (NZ - 1) + step) * SUBS + sub
        return pltpu.make_async_remote_copy(
            src_ref=src,
            dst_ref=rsb.at[way, step, pl.ds(sub * ROWS, ROWS)],
            send_sem=r_send.at[index],
            recv_sem=r_recv.at[index],
            device_id=at_z(z + 1) if way == 0 else at_z(z + NZ - 1),
            device_id_type=pl.DeviceIdType.MESH,
        )

    def block_of(way, step):
        return (z - 1 - step + 2 * NZ) % NZ if way == 0 else (z + 1 + step) % NZ

    def local(way, step, sub):
        return pt.at[block_of(way, step), pl.ds(way * COLS + sub * ROWS, ROWS)]

    project(z + NZ - 1)
    for sub in range(SUBS):
        ring.append(ring_copy(0, 0, sub, local(0, 0, sub)))
        ring[-1].start()
    project(z + 1)
    for sub in range(SUBS):
        ring.append(ring_copy(1, 0, sub, local(1, 0, sub)))
        ring[-1].start()
    for step in (2, 6, 3, 5, 4, 0):
        project(z + step)
    for step in range(1, NZ):
        for sub in range(SUBS):
            for way in range(2):
                index = ring_copy(way, step - 1, sub, local(way, 0, sub))
                index.wait_recv()
                place = rsb.at[way, step - 1, pl.ds(sub * ROWS, ROWS)]
                total = place[...] + local(way, step, sub)[...]
                if step < NZ - 1:
                    place[...] = total
                    ring.append(ring_copy(way, step, sub, place))
                    ring[-1].start()
                else:
                    fin[way, pl.ds(sub * ROWS, ROWS)] = total
    last = pltpu.make_async_remote_copy(
        src_ref=fin.at[1 - ylo],
        dst_ref=fin_rx,
        send_sem=y_send,
        recv_sem=y_recv,
        device_id={"head": z * 2 + 1 - ylo},
        device_id_type=pl.DeviceIdType.MESH,
    )
    last.start()
    last.wait_recv()
    out_ref[...] = fin[ylo] + fin_rx[...]
    for one in swaps + sends + [swap] + ring + [last]:
        one.wait_send()


def body(
    query_share, key_share, value_share, query_mask, key_mask, value_mask,
    score_triple, square_triple, weight_mask, output_triple, out_weight,
):
    dma = pltpu.SemaphoreType.DMA
    result = pl.pallas_call(
        kernel,
        out_shape=jax.ShapeDtypeStruct((COLS, T), F32),
        in_specs=[pl.BlockSpec(memory_space=pl.ANY)] * 11,
        out_specs=pl.BlockSpec(memory_space=pltpu.VMEM),
        scratch_shapes=[
            pltpu.VMEM((4, 2, T, T), BF16),
            pltpu.VMEM((3, 2, T, T), BF16),
            pltpu.VMEM((3, 2, T, SLOTS * T), BF16),
            pltpu.VMEM((2 * T, 16 * COLS), BF16),
            pltpu.VMEM((16 * COLS, 2 * T), BF16),
            pltpu.VMEM((SLOTS, 8, T, T), BF16),
            pltpu.VMEM((T, 6 * T), BF16),
            pltpu.VMEM((2, T, T), F32),
            pltpu.VMEM((2, T, T), F32),
            pltpu.VMEM((NZ, 2 * COLS, T), F32),
            pltpu.VMEM((2, NZ - 1, COLS, T), F32),
            pltpu.VMEM((2, COLS, T), F32),
            pltpu.VMEM((COLS, T), F32),
            dma((10,)),
            dma((10,)),
            dma((10,)),
            dma,
            dma((64,)),
            dma((64,)),
            dma,
            dma,
            dma((2 * (NZ - 1) * SUBS,)),
            dma((2 * (NZ - 1) * SUBS,)),
            dma,
            dma,
        ],
        compiler_params=pltpu.CompilerParams(
            collective_id=0, has_side_effects=True, vmem_limit_bytes=40 * 1024 * 1024
        ),
    )(
        key_share, key_mask, value_share, value_mask, query_share, query_mask, output_triple,
        score_triple, square_triple, weight_mask, out_weight,
    )
    return result.T[None]


def solution(mesh):
    shares = P("party", "head", "seq", None)
    return jax.shard_map(
        body,
        mesh=mesh,
        in_specs=(shares,) * 10 + (P("head", None),),
        out_specs=P("party", "seq", "head"),
        check_vma=False,
    )
```

```python
import functools

import jax
import jax.numpy as jnp
from jax import lax
from jax.experimental import pallas as pl
from jax.experimental.pallas import tpu as pltpu
from jax.sharding import PartitionSpec as P

F32 = jnp.float32
BF16 = jnp.bfloat16
T = 128
NX, NY, NZ = 4, 4, 8
SLOTS = NX * NY
COLS = 160
SCALES = 5 * T
BLOCK = SCALES + 16
CHUNKS = ((0, 256, True, 1), (256, 256, True, -1), (512, 80, False, 1), (592, 64, False, -1))
POWER = 16
HEADS = [(dz, other) for dz in (4, 3, 5, 2, 6, 1, 7, 0) for other in (0, 1) if dz or other]
TOP = 2.0 ** (126 / POWER)


def split(value):
    high = value.astype(BF16)
    return high, (value - high.astype(F32)).astype(BF16)


def scale_of(value):
    top = jnp.maximum(jnp.max(jnp.abs(value), axis=0, keepdims=True), 1e-30)
    return (top * 1.01).astype(BF16).astype(F32)


def encode(value, scale):
    code = jnp.abs(value) * (TOP / scale)
    for _ in range(4):
        code = code * code
    return jnp.where(value < 0, -code, code).astype(BF16)


def decode(code, scale):
    code = code.astype(F32)
    size = jnp.exp2(jnp.log2(jnp.maximum(jnp.abs(code), 2.0**-126)) * (1 / POWER)) * (scale / TOP)
    return jnp.where(code < 0, -size, size)


def nt(left, right):
    return lax.dot_general(left, right, (((1,), (1,)), ((), ())), preferred_element_type=F32)


def nn(left, right):
    return lax.dot_general(left, right, (((1,), (0,)), ((), ())), preferred_element_type=F32)


def kernel(
    ks, km, vs, vm, qs, qm, ot, zt, st, wm, ow, out_ref,
    kv, qo, big, wt_in, wt, gat, qa, acc, outs, tx, rx,
    loc_sem, swp_send, swp_recv, w_sem, g_send, g_recv, h_send, h_recv, r_send, r_recv,
):
    party = lax.axis_index("party")
    head = lax.axis_index("head")
    seq = lax.axis_index("seq")
    z, ylo = head // 2, head % 2
    yh, x = seq // NX, seq % NX
    sib = {"party": 1 - party}

    def at_slot(y, xx):
        return (y % NY) * NX + xx % NX

    def at_head(dz, other):
        return {"head": ((z + dz) % NZ) * 2 + (1 - ylo if other else ylo)}

    peers = [
        sib,
        {"seq": at_slot(yh, x + 1)},
        {"seq": at_slot(yh, x + NX - 1)},
        {"seq": at_slot(yh + 1, x)},
        {"seq": at_slot(yh + NY - 1, x)},
    ] + [at_head(dz, other) for dz, other in HEADS]
    barrier = pltpu.get_barrier_semaphore()
    for peer in peers:
        pl.semaphore_signal(barrier, inc=1, device_id=peer, device_id_type=pl.DeviceIdType.MESH)

    arrays = [ks, km, vs, vm, qs, qm, ot, zt, st, wm]
    places = [kv.at[i] for i in range(4)] + [qo.at[i] for i in range(3)] + [big.at[i] for i in range(3)]
    locals_ = []
    for i, (src, dst) in enumerate(zip(arrays, places)):
        locals_.append(pltpu.make_async_copy(src.at[0, party], dst.at[party], loc_sem.at[i]))
        locals_[-1].start()
    weights_in = pltpu.make_async_copy(ow, wt_in, w_sem)
    weights_in.start()
    pl.semaphore_wait(barrier, len(peers))
    swaps = []
    for i, (src, dst) in enumerate(zip(arrays, places)):
        swaps.append(
            pltpu.make_async_remote_copy(
                src_ref=src.at[0, 1 - party],
                dst_ref=dst.at[party],
                send_sem=swp_send.at[i],
                recv_sem=swp_recv.at[i],
                device_id=sib,
                device_id_type=pl.DeviceIdType.MESH,
            )
        )
        swaps[-1].start()

    def arrived(i):
        locals_[i].wait()
        swaps[i].wait_recv()

    for i in range(4):
        arrived(i)

    def wide(ref):
        return ref[...].astype(F32)

    k = wide(kv.at[0, 0]) + wide(kv.at[0, 1])
    b = wide(kv.at[1, 0]) + wide(kv.at[1, 1])
    d = (wide(kv.at[2, 0]) - wide(kv.at[3, 0])) + (wide(kv.at[2, 1]) - wide(kv.at[3, 1]))
    scales = [scale_of(value) for value in (k, b, d)]
    for i, value in enumerate((k, b, d)):
        gat[seq, i * T : (i + 1) * T] = encode(value, scales[i])
    gat[seq, 3 * T : 4 * T] = kv[3, 0]
    gat[seq, 4 * T : 5 * T] = kv[3, 1]
    row = lax.broadcasted_iota(jnp.int32, (16, T), 0)
    gat[seq, SCALES:] = jnp.where(row == 0, scales[0], jnp.where(row == 1, scales[1], scales[2])).astype(BF16)

    sends = []

    def copy(chunk, first, second, y, xx, target):
        start, count = CHUNKS[chunk][:2]
        place = gat.at[at_slot(y, xx), pl.ds(start, count)]
        return pltpu.make_async_remote_copy(
            src_ref=place,
            dst_ref=place,
            send_sem=g_send.at[chunk * 16 + first * 4 + second],
            recv_sem=g_recv.at[chunk * 16 + first * 4 + second],
            device_id={"seq": target},
            device_id_type=pl.DeviceIdType.MESH,
        )

    def send(chunk, first, second, y, xx, along_y, step):
        target = at_slot(yh + step + NY, x) if along_y else at_slot(yh, x + step + NX)
        one = copy(chunk, first, second, y, xx, target)
        one.start()
        sends.append(one)

    def origin(chunk, first, second):
        _, _, y_first, sign = CHUNKS[chunk]
        moves = (0, -sign, sign, 2)
        dy, dx = (moves[first], moves[second]) if y_first else (moves[second], moves[first])
        return yh + dy + NY, x + dx + NX

    def spread_second(chunk, first):
        _, _, y_first, sign = CHUNKS[chunk]
        y, xx = origin(chunk, first, 0)
        send(chunk, first, 1, y, xx, not y_first, sign)
        send(chunk, first, 2, y, xx, not y_first, -sign)

    def receive(chunk, first, second):
        _, _, y_first, sign = CHUNKS[chunk]
        y, xx = origin(chunk, first, second)
        copy(chunk, first, second, y, xx, seq).wait_recv()
        if second == 0:
            if first == 1:
                send(chunk, 3, 0, y, xx, y_first, sign)
            spread_second(chunk, first)
        elif second == 1:
            send(chunk, first, 3, y, xx, not y_first, sign)

    for chunk, (_, _, y_first, sign) in enumerate(CHUNKS):
        send(chunk, 1, 0, yh, x, y_first, sign)
        send(chunk, 2, 0, yh, x, y_first, -sign)
    for chunk in range(4):
        spread_second(chunk, 0)

    for i in range(4, 7):
        arrived(i)
    scale = T ** (-0.5)
    qh, ql = split(scale * (wide(qo.at[0, 0]) + wide(qo.at[0, 1])))
    ah, al = split(-scale * (wide(qo.at[1, 0]) + wide(qo.at[1, 1])))
    for i, value in enumerate((qh, qh, ql, ah, ah, al)):
        qa[:, i * T : (i + 1) * T] = value
    acc[0] = wide(qo.at[2, 0])
    acc[1] = wide(qo.at[2, 1])
    for i in range(7, 10):
        arrived(i)

    def attend(slot):
        cols = pl.ds(pl.multiple_of(slot * T, T), T)
        scales = gat[slot, SCALES:].astype(F32)
        (kh, kl), (bh, bl), (dh, dl) = [
            split(decode(gat[slot, i * T : (i + 1) * T], scales[i : i + 1])) for i in range(3)
        ]
        c0 = gat[slot, 3 * T : 4 * T]
        c1 = gat[slot, 4 * T : 5 * T]
        scores = nt(qa[...], jnp.concatenate([kh, kl, kh, bh, bl, bh], axis=1))
        zz = big[0, 0, :, cols].astype(F32) + big[0, 1, :, cols].astype(F32)
        sq = big[1, 0, :, cols].astype(F32) + big[1, 1, :, cols].astype(F32)
        w0 = big[2, 0, :, cols]
        w1 = big[2, 1, :, cols]
        poly = 1.25 + zz + 0.25 * sq + scores * (1.0 + 0.5 * zz + 0.25 * scores)
        row = seq * T + lax.broadcasted_iota(jnp.int32, (T, T), 0)
        col = slot * T + lax.broadcasted_iota(jnp.int32, (T, T), 1)
        weights = jnp.where(col <= row, poly * lax.rsqrt((row + 1).astype(F32)), 0.0)
        lead = weights - w1.astype(F32)
        opened = lead - w0.astype(F32)
        lh, ll = split(lead)
        oh, ol = split(opened)
        both = jnp.concatenate([c0, c1], axis=1)
        mixed = nn(jnp.concatenate([oh, ol], axis=1), jnp.concatenate([both, both], axis=0))
        acc[0] += mixed[:, :T] + nn(
            jnp.concatenate([lh, ll, lh], axis=1), jnp.concatenate([dh, dh, dl], axis=0)
        )
        acc[1] += mixed[:, T:] + nn(
            jnp.concatenate([w1, w1], axis=1), jnp.concatenate([dh, dl], axis=0)
        )

    def attend_at(dy, dx):
        attend(at_slot(yh + dy + NY, x + dx + NX))

    weights_in.wait()

    @pl.loop(0, 20)
    def _(i):
        cols = pl.ds(pl.multiple_of(i * T, T), T)
        wt[cols, :] = wt_in[:, cols].T

    attend_at(0, 0)
    for chunk in range(4):
        receive(chunk, 1, 0)
    for chunk in range(4):
        receive(chunk, 2, 0)
    for chunk in range(4):
        receive(chunk, 0, 1)
    for chunk in range(4):
        receive(chunk, 0, 2)
    for dy, dx in ((1, 0), (-1, 0), (0, 1), (0, -1)):
        attend_at(dy, dx)
    for chunk in range(4):
        receive(chunk, 3, 0)
    for chunk in range(4):
        receive(chunk, 1, 1)
        receive(chunk, 2, 1)
    for chunk in range(4):
        receive(chunk, 0, 3)
        receive(chunk, 1, 2)
        receive(chunk, 2, 2)
        receive(chunk, 3, 1)
    for dy, dx in ((2, 0), (0, 2), (1, 1), (1, -1), (-1, 1), (-1, -1)):
        attend_at(dy, dx)
    for chunk in range(4):
        receive(chunk, 3, 2)
        receive(chunk, 1, 3)
        receive(chunk, 2, 3)
    for dy, dx in ((2, 1), (2, -1), (1, 2), (-1, 2)):
        attend_at(dy, dx)
    for chunk in range(4):
        receive(chunk, 3, 3)
    attend_at(2, 2)

    swap = pltpu.make_async_remote_copy(
        src_ref=acc.at[1 - party],
        dst_ref=outs.at[party],
        send_sem=h_send,
        recv_sem=h_recv,
        device_id=sib,
        device_id_type=pl.DeviceIdType.MESH,
    )
    swap.start()
    outs[party] = acc[party]
    swap.wait_recv()
    oh, ol = split(jnp.concatenate([outs[0], outs[1]], axis=1))
    ohl = jnp.concatenate([oh, ol], axis=1)

    def project(dz, other):
        target = ((z + dz) % NZ) * 2 + (1 - ylo if other else ylo)
        part = wt[pl.ds(pl.multiple_of(target * COLS, COLS), COLS), :]
        return nt(jnp.concatenate([part, part], axis=1), ohl)

    out_sends = []
    for i, (dz, other) in enumerate(HEADS):
        value = project(dz, other)
        scale = scale_of(value)
        tx[i, :COLS] = encode(value, scale)
        tx[i, COLS:] = jnp.broadcast_to(scale, (16, T)).astype(BF16)
        out_sends.append(
            pltpu.make_async_remote_copy(
                src_ref=tx.at[i],
                dst_ref=rx.at[i],
                send_sem=r_send.at[i],
                recv_sem=r_recv.at[i],
                device_id=at_head(dz, other),
                device_id_type=pl.DeviceIdType.MESH,
            )
        )
        out_sends[-1].start()
    total = project(0, 0)
    for i, one in enumerate(out_sends):
        one.wait_recv()
        total += decode(rx[i, :COLS], rx[i, COLS:][:1].astype(F32))
    out_ref[...] = total
    for one in swaps + sends + [swap] + out_sends:
        one.wait_send()


def body(
    query_share, key_share, value_share, query_mask, key_mask, value_mask,
    score_triple, square_triple, weight_mask, output_triple, out_weight,
):
    dma = pltpu.SemaphoreType.DMA
    result = pl.pallas_call(
        kernel,
        out_shape=jax.ShapeDtypeStruct((COLS, T), F32),
        in_specs=[pl.BlockSpec(memory_space=pl.ANY)] * 11,
        out_specs=pl.BlockSpec(memory_space=pltpu.VMEM),
        scratch_shapes=[
            pltpu.VMEM((4, 2, T, T), BF16),
            pltpu.VMEM((3, 2, T, T), BF16),
            pltpu.VMEM((3, 2, T, SLOTS * T), BF16),
            pltpu.VMEM((2 * T, 16 * COLS), BF16),
            pltpu.VMEM((16 * COLS, 2 * T), BF16),
            pltpu.VMEM((SLOTS, BLOCK, T), BF16),
            pltpu.VMEM((T, 6 * T), BF16),
            pltpu.VMEM((2, T, T), F32),
            pltpu.VMEM((2, T, T), F32),
            pltpu.VMEM((len(HEADS), COLS + 16, T), BF16),
            pltpu.VMEM((len(HEADS), COLS + 16, T), BF16),
            dma((10,)),
            dma((10,)),
            dma((10,)),
            dma,
            dma((64,)),
            dma((64,)),
            dma,
            dma,
            dma((len(HEADS),)),
            dma((len(HEADS),)),
        ],
        compiler_params=pltpu.CompilerParams(
            collective_id=0, has_side_effects=True, vmem_limit_bytes=60 * 1024 * 1024
        ),
    )(
        key_share, key_mask, value_share, value_mask, query_share, query_mask, output_triple,
        score_triple, square_triple, weight_mask, out_weight,
    )
    return result.T[None]


def solution(mesh):
    shares = P("party", "head", "seq", None)
    return jax.shard_map(
        body,
        mesh=mesh,
        in_specs=(shares,) * 10 + (P("head", None),),
        out_specs=P("party", "seq", "head"),
        check_vma=False,
    )
```

```python
import functools

import jax
import jax.numpy as jnp
from jax import lax
from jax.experimental import pallas as pl
from jax.experimental.pallas import tpu as pltpu
from jax.sharding import PartitionSpec as P

F32 = jnp.float32
BF16 = jnp.bfloat16
T = 128
NX, NY, NZ = 4, 4, 8
SLOTS = NX * NY
COLS = 160
SCALES = 5 * T
BLOCK = SCALES + 16
CHUNKS = ((0, 256, True, 1), (256, 256, True, -1), (512, 80, False, 1), (592, 64, False, -1))
POWER = 16
STEPS = (4, 3, 5, 2, 6, 1, 7, 0)
TOP = 2.0 ** (126 / POWER)


def split(value):
    high = value.astype(BF16)
    return high, (value - high.astype(F32)).astype(BF16)


def scale_of(value):
    top = jnp.maximum(jnp.max(jnp.abs(value), axis=0, keepdims=True), 1e-30)
    return (top * 1.01).astype(BF16).astype(F32)


def encode(value, scale):
    code = jnp.abs(value) * (TOP / scale)
    for _ in range(4):
        code = code * code
    return jnp.where(value < 0, -code, code).astype(BF16)


def decode(code, scale):
    code = code.astype(F32)
    size = jnp.exp2(jnp.log2(jnp.maximum(jnp.abs(code), 2.0**-126)) * (1 / POWER)) * (scale / TOP)
    return jnp.where(code < 0, -size, size)


def nt(left, right):
    return lax.dot_general(left, right, (((1,), (1,)), ((), ())), preferred_element_type=F32)


def nn(left, right):
    return lax.dot_general(left, right, (((1,), (0,)), ((), ())), preferred_element_type=F32)


def kernel(
    ks, km, vs, vm, qs, qm, ot, zt, st, wm, ow, out_ref,
    kv, qo, big, wt_in, wt, gat, qa, acc, outs, ty, ry, tz, rz,
    loc_sem, swp_send, swp_recv, w_sem, g_send, g_recv, h_send, h_recv, y_send, y_recv, z_send, z_recv, round_1, round_2,
):
    party = lax.axis_index("party")
    head = lax.axis_index("head")
    seq = lax.axis_index("seq")
    z, ylo = head // 2, head % 2
    yh, x = seq // NX, seq % NX
    sib = {"party": 1 - party}

    def at_slot(y, xx):
        return (y % NY) * NX + xx % NX

    def at_z(dz):
        return {"head": ((z + dz) % NZ) * 2 + ylo}

    pair = {"head": z * 2 + 1 - ylo}
    peers = [
        sib,
        {"seq": at_slot(yh, x + 1)},
        {"seq": at_slot(yh, x + NX - 1)},
        {"seq": at_slot(yh + 1, x)},
        {"seq": at_slot(yh + NY - 1, x)},
        at_z(1),
        at_z(NZ - 1),
        pair,
    ]

    def tell(semaphore, peer):
        pl.semaphore_signal(semaphore, inc=1, device_id=peer, device_id_type=pl.DeviceIdType.MESH)

    barrier = pltpu.get_barrier_semaphore()
    for peer in peers:
        tell(barrier, peer)

    arrays = [ks, km, vs, vm, qs, qm, ot, zt, st, wm]
    places = [kv.at[i] for i in range(4)] + [qo.at[i] for i in range(3)] + [big.at[i] for i in range(3)]
    locals_ = []
    for i, (src, dst) in enumerate(zip(arrays, places)):
        locals_.append(pltpu.make_async_copy(src.at[0, party], dst.at[party], loc_sem.at[i]))
        locals_[-1].start()
    weights_in = pltpu.make_async_copy(ow, wt_in, w_sem)
    weights_in.start()
    pl.semaphore_wait(barrier, len(peers))
    swaps = []
    for i, (src, dst) in enumerate(zip(arrays, places)):
        swaps.append(
            pltpu.make_async_remote_copy(
                src_ref=src.at[0, 1 - party],
                dst_ref=dst.at[party],
                send_sem=swp_send.at[i],
                recv_sem=swp_recv.at[i],
                device_id=sib,
                device_id_type=pl.DeviceIdType.MESH,
            )
        )
        swaps[-1].start()

    tell(round_1, at_z(1))
    tell(round_1, at_z(NZ - 1))

    def arrived(i):
        locals_[i].wait()
        swaps[i].wait_recv()

    def wide(ref):
        return ref[...].astype(F32)

    sends = []

    def copy(chunk, first, second, y, xx, target):
        start, count = CHUNKS[chunk][:2]
        place = gat.at[at_slot(y, xx), pl.ds(start, count)]
        return pltpu.make_async_remote_copy(
            src_ref=place,
            dst_ref=place,
            send_sem=g_send.at[chunk * 16 + first * 4 + second],
            recv_sem=g_recv.at[chunk * 16 + first * 4 + second],
            device_id={"seq": target},
            device_id_type=pl.DeviceIdType.MESH,
        )

    def send(chunk, first, second, y, xx, along_y, step):
        target = at_slot(yh + step + NY, x) if along_y else at_slot(yh, x + step + NX)
        one = copy(chunk, first, second, y, xx, target)
        one.start()
        sends.append(one)

    def origin(chunk, first, second):
        _, _, y_first, sign = CHUNKS[chunk]
        moves = (0, -sign, sign, 2)
        dy, dx = (moves[first], moves[second]) if y_first else (moves[second], moves[first])
        return yh + dy + NY, x + dx + NX

    def spread_second(chunk, first):
        _, _, y_first, sign = CHUNKS[chunk]
        y, xx = origin(chunk, first, 0)
        send(chunk, first, 1, y, xx, not y_first, sign)
        send(chunk, first, 2, y, xx, not y_first, -sign)

    received = set()

    def receive(chunk, first, second):
        if (chunk, first, second) in received or first == second == 0:
            return
        received.add((chunk, first, second))
        _, _, y_first, sign = CHUNKS[chunk]
        y, xx = origin(chunk, first, second)
        copy(chunk, first, second, y, xx, seq).wait_recv()
        if second == 0:
            if first == 1:
                send(chunk, 3, 0, y, xx, y_first, sign)
            spread_second(chunk, first)
        elif second == 1:
            send(chunk, first, 3, y, xx, not y_first, sign)

    def spread_first(chunk, first):
        _, _, y_first, sign = CHUNKS[chunk]
        send(chunk, first, 0, yh, x, y_first, sign if first == 1 else -sign)

    scales = []

    def place(i, value):
        scales.append(scale_of(value))
        gat[seq, i * T : (i + 1) * T] = encode(value, scales[i])

    arrived(0)
    arrived(1)
    place(0, wide(kv.at[0, 0]) + wide(kv.at[0, 1]))
    place(1, wide(kv.at[1, 0]) + wide(kv.at[1, 1]))
    spread_first(0, 1)
    spread_first(0, 2)
    spread_second(0, 0)
    arrived(2)
    arrived(3)
    place(2, (wide(kv.at[2, 0]) - wide(kv.at[3, 0])) + (wide(kv.at[2, 1]) - wide(kv.at[3, 1])))
    gat[seq, 3 * T : 4 * T] = kv[3, 0]
    spread_first(1, 1)
    spread_first(1, 2)
    spread_second(1, 0)
    gat[seq, 4 * T : 5 * T] = kv[3, 1]
    row = lax.broadcasted_iota(jnp.int32, (16, T), 0)
    gat[seq, SCALES:] = jnp.where(row == 0, scales[0], jnp.where(row == 1, scales[1], scales[2])).astype(BF16)
    for chunk in (2, 3):
        spread_first(chunk, 1)
        spread_first(chunk, 2)

    for i in range(4, 7):
        arrived(i)
    scale = T ** (-0.5)
    qh, ql = split(scale * (wide(qo.at[0, 0]) + wide(qo.at[0, 1])))
    ah, al = split(-scale * (wide(qo.at[1, 0]) + wide(qo.at[1, 1])))
    for i, value in enumerate((qh, qh, ql, ah, ah, al)):
        qa[:, i * T : (i + 1) * T] = value
    acc[0] = wide(qo.at[2, 0])
    acc[1] = wide(qo.at[2, 1])
    for i in range(7, 10):
        arrived(i)

    def attend(slot):
        cols = pl.ds(pl.multiple_of(slot * T, T), T)
        scales = gat[slot, SCALES:].astype(F32)
        (kh, kl), (bh, bl), (dh, dl) = [
            split(decode(gat[slot, i * T : (i + 1) * T], scales[i : i + 1])) for i in range(3)
        ]
        c0 = gat[slot, 3 * T : 4 * T]
        c1 = gat[slot, 4 * T : 5 * T]
        scores = nt(qa[...], jnp.concatenate([kh, kl, kh, bh, bl, bh], axis=1))
        zz = big[0, 0, :, cols].astype(F32) + big[0, 1, :, cols].astype(F32)
        sq = big[1, 0, :, cols].astype(F32) + big[1, 1, :, cols].astype(F32)
        w0 = big[2, 0, :, cols]
        w1 = big[2, 1, :, cols]
        poly = 1.25 + zz + 0.25 * sq + scores * (1.0 + 0.5 * zz + 0.25 * scores)
        row = seq * T + lax.broadcasted_iota(jnp.int32, (T, T), 0)
        col = slot * T + lax.broadcasted_iota(jnp.int32, (T, T), 1)
        weights = jnp.where(col <= row, poly * lax.rsqrt((row + 1).astype(F32)), 0.0)
        lead = weights - w1.astype(F32)
        opened = lead - w0.astype(F32)
        lh, ll = split(lead)
        oh, ol = split(opened)
        both = jnp.concatenate([c0, c1], axis=1)
        mixed = nn(jnp.concatenate([oh, ol], axis=1), jnp.concatenate([both, both], axis=0))
        acc[0] += mixed[:, :T] + nn(
            jnp.concatenate([lh, ll, lh], axis=1), jnp.concatenate([dh, dh, dl], axis=0)
        )
        acc[1] += mixed[:, T:] + nn(
            jnp.concatenate([w1, w1], axis=1), jnp.concatenate([dh, dl], axis=0)
        )

    def attend_at(dy, dx):
        for chunk, (_, _, y_first, sign) in enumerate(CHUNKS):
            moves = (0, -sign, sign, 2)
            first, second = (dy, dx) if y_first else (dx, dy)
            receive(chunk, moves.index(first), moves.index(second))
        attend(at_slot(yh + dy + NY, x + dx + NX))

    weights_in.wait()

    @pl.loop(0, 20)
    def _(i):
        cols = pl.ds(pl.multiple_of(i * T, T), T)
        wt[cols, :] = wt_in[:, cols].T

    def receive_all(chunks, first, second):
        for chunk in chunks:
            receive(chunk, first, second)

    AB, CD = (0, 1), (2, 3)
    receive_all(AB, 0, 1)
    receive_all(AB, 1, 0)
    receive_all(AB, 2, 0)
    for chunk in CD:
        spread_second(chunk, 0)
    receive_all(CD, 1, 0)
    receive_all(CD, 2, 0)
    pl.semaphore_wait(round_1, 2)
    tell(round_2, at_z(2))
    tell(round_2, at_z(NZ - 2))
    attend_at(0, 0)
    receive_all(AB, 1, 1)
    receive_all(AB, 2, 1)
    receive_all(AB, 3, 0)
    receive_all(CD, 0, 1)
    receive_all(CD, 3, 0)
    attend_at(0, 1)
    attend_at(0, -1)
    receive_all(CD, 1, 1)
    receive_all(CD, 2, 1)
    receive_all(AB, 3, 1)
    attend_at(1, 0)
    attend_at(-1, 0)
    receive_all(CD, 3, 1)
    attend_at(0, 2)
    attend_at(2, 0)
    for dy, dx in ((1, 1), (1, -1), (-1, 1), (-1, -1)):
        attend_at(dy, dx)
    pl.semaphore_wait(round_2, 2)
    for dy, dx in ((1, 2), (-1, 2), (2, 1), (2, -1), (2, 2)):
        attend_at(dy, dx)

    swap = pltpu.make_async_remote_copy(
        src_ref=acc.at[1 - party],
        dst_ref=outs.at[party],
        send_sem=h_send,
        recv_sem=h_recv,
        device_id=sib,
        device_id_type=pl.DeviceIdType.MESH,
    )
    swap.start()
    outs[party] = acc[party]
    swap.wait_recv()
    oh, ol = split(jnp.concatenate([outs[0], outs[1]], axis=1))
    ohl = jnp.concatenate([oh, ol], axis=1)

    def project(dz, column):
        target = ((z + dz) % NZ) * 2 + column
        part = wt[pl.ds(pl.multiple_of(target * COLS, COLS), COLS), :]
        return nt(jnp.concatenate([part, part], axis=1), ohl)

    out_sends = []

    def pass_on(value, i, src, dst, sends_sem, recvs_sem, peer):
        scale = scale_of(value)
        src[i, :COLS] = encode(value, scale)
        src[i, COLS:] = jnp.broadcast_to(scale, (16, T)).astype(BF16)
        out_sends.append(
            pltpu.make_async_remote_copy(
                src_ref=src.at[i],
                dst_ref=dst.at[i],
                send_sem=sends_sem.at[i],
                recv_sem=recvs_sem.at[i],
                device_id=peer,
                device_id_type=pl.DeviceIdType.MESH,
            )
        )
        out_sends[-1].start()
        return out_sends[-1]

    def incoming(ref, i):
        return decode(ref[i, :COLS], ref[i, COLS:][:1].astype(F32))

    from_pair = [
        pass_on(project(dz, 1 - ylo), i, ty, ry, y_send, y_recv, pair) for i, dz in enumerate(STEPS)
    ]
    from_z = []
    for i, dz in enumerate(STEPS):
        value = project(dz, ylo)
        from_pair[i].wait_recv()
        value += incoming(ry, i)
        if dz:
            from_z.append(pass_on(value, i, tz, rz, z_send, z_recv, at_z(dz)))
    for i, one in enumerate(from_z):
        one.wait_recv()
        value += incoming(rz, i)
    out_ref[...] = value
    for one in swaps + sends + [swap] + out_sends:
        one.wait_send()


def body(
    query_share, key_share, value_share, query_mask, key_mask, value_mask,
    score_triple, square_triple, weight_mask, output_triple, out_weight,
):
    dma = pltpu.SemaphoreType.DMA
    result = pl.pallas_call(
        kernel,
        out_shape=jax.ShapeDtypeStruct((COLS, T), F32),
        in_specs=[pl.BlockSpec(memory_space=pl.ANY)] * 11,
        out_specs=pl.BlockSpec(memory_space=pltpu.VMEM),
        scratch_shapes=[
            pltpu.VMEM((4, 2, T, T), BF16),
            pltpu.VMEM((3, 2, T, T), BF16),
            pltpu.VMEM((3, 2, T, SLOTS * T), BF16),
            pltpu.VMEM((2 * T, 16 * COLS), BF16),
            pltpu.VMEM((16 * COLS, 2 * T), BF16),
            pltpu.VMEM((SLOTS, BLOCK, T), BF16),
            pltpu.VMEM((T, 6 * T), BF16),
            pltpu.VMEM((2, T, T), F32),
            pltpu.VMEM((2, T, T), F32),
            pltpu.VMEM((NZ, COLS + 16, T), BF16),
            pltpu.VMEM((NZ, COLS + 16, T), BF16),
            pltpu.VMEM((NZ - 1, COLS + 16, T), BF16),
            pltpu.VMEM((NZ - 1, COLS + 16, T), BF16),
            dma((10,)),
            dma((10,)),
            dma((10,)),
            dma,
            dma((64,)),
            dma((64,)),
            dma,
            dma,
            dma((NZ,)),
            dma((NZ,)),
            dma((NZ - 1,)),
            dma((NZ - 1,)),
            pltpu.SemaphoreType.REGULAR,
            pltpu.SemaphoreType.REGULAR,
        ],
        compiler_params=pltpu.CompilerParams(
            collective_id=0, has_side_effects=True, vmem_limit_bytes=60 * 1024 * 1024
        ),
    )(
        key_share, key_mask, value_share, value_mask, query_share, query_mask, output_triple,
        score_triple, square_triple, weight_mask, out_weight,
    )
    return result.T[None]


def solution(mesh):
    shares = P("party", "head", "seq", None)
    return jax.shard_map(
        body,
        mesh=mesh,
        in_specs=(shares,) * 10 + (P("head", None),),
        out_specs=P("party", "seq", "head"),
        check_vma=False,
    )
```

```python
import functools

import jax
import jax.numpy as jnp
from jax import lax
from jax.experimental import pallas as pl
from jax.experimental.pallas import tpu as pltpu
from jax.sharding import PartitionSpec as P

F32 = jnp.float32
BF16 = jnp.bfloat16
T = 128
NX, NY, NZ = 4, 4, 8
SLOTS = NX * NY
REL = {0: 0, -1: 1, 1: 2, 2: 3, -2: 3}
COLS = 160
K, B, SCALES, D, C0, C1 = 0, T, 2 * T, 2 * T + 16, 3 * T + 16, 4 * T + 16
BLOCK = 5 * T + 16
CHUNKS = ((0, 272, True, 1), (272, 272, True, -1), (544, 64, False, 1), (608, 48, False, -1))
ORDER = (
    ("y", 0, -1),
    ("y", 1, 1),
    ("x", 3, 1),
    ("yx", 0, 0, -1),
    ("yx", 1, 0, 1),
    ("x", 2, 1),
    ("x", 3, -1),
    ("x", 2, -1),
    ("x", 3, 2),
    ("y", 1, -1),
    ("yx", 1, 0, -1),
    ("yx", 0, 0, 1),
    ("y", 0, 1),
    ("yx", 0, 0, 2),
    ("x", 2, 2),
    ("yx", 1, 0, 2),
    ("y", 1, 2),
    ("yx", 0, -1, 1),
    ("y", 0, 2),
    ("yx", 1, 1, -1),
    ("yx", 1, 1, 1),
    ("yx", 0, -1, -1),
    ("turn",),
    ("yx", 1, -1, 1),
    ("xy", 3, "rest", 1),
    ("yx", 0, 1, -1),
    ("xy", 2, "own", -1),
    ("xy", 2, "rest", -1),
    ("query",),
    ("yx", 0, 1, 1),
    ("yx", 1, -1, -1),
    ("xy", 3, "own", 1),
    ("attend", 0, 1),
    ("xy", 2, "rest", 1),
    ("yx", 1, 1, 2),
    ("yx", 0, 2, -1),
    ("xy", 3, "own", -1),
    ("attend", 0, -1),
    ("xy", 3, "rest", -1),
    ("attend", 0, 2),
    ("yx", 0, 1, 2),
    ("yx", 1, 2, 1),
    ("attend", 0, 0),
    ("xy", 2, "own", 1),
    ("yx", 1, 2, -1),
    ("xy", 2, "own", 2),
    ("xy", 3, "own", 2),
    ("yx", 1, -1, 2),
    ("xy", 2, "rest", 2),
    ("xy", 3, "rest", 2),
    ("yx", 0, -1, 2),
    ("attend", -1, 0),
    ("yx", 0, 2, 1),
    ("attend", 1, -1),
    ("yx", 0, 2, 2),
    ("attend", 1, 1),
    ("attend", -1, -1),
    ("yx", 1, 2, 2),
    ("attend", 2, 0),
    ("attend", 1, 2),
    ("attend", -1, 1),
    ("attend", 1, 0),
    ("attend", 2, 1),
    ("attend", 2, -1),
    ("attend", -1, 2),
    ("attend", 2, 2),
)
GROUPS = {"all": (0, 4), "own": (0, 1), "rest": (1, 3)}
SPLIT = {0: "own", 1: "rest", -1: "rest", 2: "rest"}
MESSAGES = sum(entry[0] in ("y", "x", "yx", "xy") for entry in ORDER)
POWER = 16
STEPS = (4, 3, 5, 2, 6, 1, 7, 0)
TOP = 2.0 ** (126 / POWER)


def split(value):
    high = value.astype(BF16)
    return high, (value - high.astype(F32)).astype(BF16)


def scale_of(value):
    top = jnp.maximum(jnp.max(jnp.abs(value), axis=0, keepdims=True), 1e-30)
    return (top * 1.01).astype(BF16).astype(F32)


def encode(value, scale):
    code = jnp.abs(value) * (TOP / scale)
    for _ in range(4):
        code = code * code
    return jnp.where(value < 0, -code, code).astype(BF16)


def decode(code, scale):
    code = code.astype(F32)
    size = jnp.exp2(jnp.log2(jnp.maximum(jnp.abs(code), 2.0**-126)) * (1 / POWER)) * (scale / TOP)
    return jnp.where(code < 0, -size, size)


def nt(left, right):
    return lax.dot_general(left, right, (((1,), (1,)), ((), ())), preferred_element_type=F32)


def nn(left, right):
    return lax.dot_general(left, right, (((1,), (0,)), ((), ())), preferred_element_type=F32)


def kernel(
    ks, km, vs, vm, qs, qm, ot, zt, st, wm, ow, out_ref,
    kv, qo, big, wt_in, wt, gat, qa, acc, outs, ty, ry, tz, rz,
    loc_sem, swp_send, swp_recv, w_sem, g_send, g_recv, h_send, h_recv, y_send, y_recv, z_send, z_recv, round_1, round_2,
):
    party = lax.axis_index("party")
    head = lax.axis_index("head")
    seq = lax.axis_index("seq")
    z, ylo = head // 2, head % 2
    yh, x = seq // NX, seq % NX
    xs = {step: lax.rem(x + step + NX, NX) for step in (0, 1, -1, 2)}
    ys = {step: lax.rem(yh + step + NY, NY) for step in (0, 1, -1, 2)}
    zs = {step: lax.rem(z + step, NZ) * 2 for step in range(NZ)}
    sib = (1 - party, head, seq)
    pair = (party, z * 2 + 1 - ylo, seq)
    along_x = {step: (party, head, yh * NX + xs[step]) for step in (1, -1)}
    along_y = {step: (party, head, ys[step] * NX + x) for step in (1, -1)}
    along_z = {step: (party, zs[step] + ylo, seq) for step in range(1, NZ)}
    peers = [
        sib, along_x[1], along_x[-1], along_y[1], along_y[-1], along_z[1], along_z[NZ - 1], pair
    ]

    def tell(semaphore, peer):
        pl.semaphore_signal(semaphore, inc=1, device_id=peer, device_id_type=pl.DeviceIdType.MESH)

    barrier = pltpu.get_barrier_semaphore()
    for peer in peers:
        tell(barrier, peer)

    arrays = [ks, km, vs, vm, qs, qm, ot, zt, st, wm]
    places = [kv.at[i] for i in range(4)] + [qo.at[i] for i in range(3)] + [big.at[i] for i in range(3)]
    locals_ = [
        pltpu.make_async_copy(src.at[0, party], dst.at[party], loc_sem.at[i])
        for i, (src, dst) in enumerate(zip(arrays, places))
    ]
    swaps = [
        pltpu.make_async_remote_copy(
            src_ref=src.at[0, 1 - party],
            dst_ref=dst.at[party],
            send_sem=swp_send.at[i],
            recv_sem=swp_recv.at[i],
            device_id=sib,
            device_id_type=pl.DeviceIdType.MESH,
        )
        for i, (src, dst) in enumerate(zip(arrays, places))
    ]
    weights_in = pltpu.make_async_copy(ow, wt_in, w_sem)
    for one in locals_[:4]:
        one.start()
    pl.semaphore_wait(barrier, len(peers))
    for one in swaps[:4]:
        one.start()

    tell(round_1, along_z[1])
    tell(round_1, along_z[NZ - 1])

    def arrived(i):
        locals_[i].wait()
        swaps[i].wait_recv()

    def wide(ref):
        return ref[...].astype(F32)

    sends = []
    copies = {}

    def message(key, chunk, y_axis, step, y_blocks, x_blocks):
        start, count = CHUNKS[chunk][:2]
        (y0, ny), (x0, nx) = y_blocks, x_blocks
        src = gat.at[pl.ds(REL[y0] if ny == 1 else y0, ny), pl.ds(REL[x0] if nx == 1 else x0, nx), pl.ds(start, count)]
        if y_axis:
            y0 = y0 - step
        else:
            x0 = x0 - step
        dst = gat.at[pl.ds(REL[y0] if ny == 1 else y0, ny), pl.ds(REL[x0] if nx == 1 else x0, nx), pl.ds(start, count)]
        index = len(copies)
        copies[key] = pltpu.make_async_remote_copy(
            src_ref=src,
            dst_ref=dst,
            send_sem=g_send.at[index],
            recv_sem=g_recv.at[index],
            device_id=along_y[step] if y_axis else along_x[step],
            device_id_type=pl.DeviceIdType.MESH,
        )
        copies[key].start()
        sends.append(copies[key])

    def deliver(key, chunk, y_axis, others, away):
        sign = CHUNKS[chunk][3]
        step = -sign if away == sign else sign
        block = (-sign if away == 2 else 0, 1)
        message(key, chunk, y_axis, step, *((block, others) if y_axis else (others, block)))

    received = set()

    def receive(*key):
        if key in received:
            return
        received.add(key)
        copies[key].wait_recv()

    scales = []

    def place(i, value):
        scales.append(scale_of(value))
        gat[0, 0, i : i + T] = encode(value, scales[-1])

    for i in range(4):
        arrived(i)
    place(K, wide(kv.at[0, 0]) + wide(kv.at[0, 1]))
    place(B, wide(kv.at[1, 0]) + wide(kv.at[1, 1]))
    place(D, (wide(kv.at[2, 0]) - wide(kv.at[3, 0])) + (wide(kv.at[2, 1]) - wide(kv.at[3, 1])))
    row = lax.broadcasted_iota(jnp.int32, (16, T), 0)
    gat[0, 0, SCALES:D] = jnp.where(row == 0, scales[0], jnp.where(row == 1, scales[1], scales[2])).astype(BF16)
    gat[0, 0, C0:C1] = kv[3, 0]
    gat[0, 0, C1:] = kv[3, 1]

    def others_in():
        weights_in.start()
        for one in locals_[4:] + swaps[4:]:
            one.start()

    def attend(dy, dx):
        slot = ys[dy] * NX + xs[dx]
        ry, rx = REL[dy], REL[dx]
        cols = pl.ds(pl.multiple_of(slot * T, T), T)
        scales = gat[ry, rx, SCALES:D].astype(F32)
        (kh, kl), (bh, bl), (dh, dl) = [
            split(decode(gat[ry, rx, start : start + T], scales[i : i + 1]))
            for i, start in enumerate((K, B, D))
        ]
        c0 = gat[ry, rx, C0:C1]
        c1 = gat[ry, rx, C1:]
        scores = nt(qa[...], jnp.concatenate([kh, kl, kh, bh, bl, bh], axis=1))
        zz = big[0, 0, :, cols].astype(F32) + big[0, 1, :, cols].astype(F32)
        sq = big[1, 0, :, cols].astype(F32) + big[1, 1, :, cols].astype(F32)
        w0 = big[2, 0, :, cols]
        w1 = big[2, 1, :, cols]
        poly = 1.25 + zz + 0.25 * sq + scores * (1.0 + 0.5 * zz + 0.25 * scores)
        row = seq * T + lax.broadcasted_iota(jnp.int32, (T, T), 0)
        col = slot * T + lax.broadcasted_iota(jnp.int32, (T, T), 1)
        weights = jnp.where(col <= row, poly * lax.rsqrt((row + 1).astype(F32)), 0.0)
        lead = weights - w1.astype(F32)
        opened = lead - w0.astype(F32)
        lh, ll = split(lead)
        oh, ol = split(opened)
        both = jnp.concatenate([c0, c1], axis=1)
        mixed = nn(jnp.concatenate([oh, ol], axis=1), jnp.concatenate([both, both], axis=0))
        acc[0] += mixed[:, :T] + nn(
            jnp.concatenate([lh, ll, lh], axis=1), jnp.concatenate([dh, dh, dl], axis=0)
        )
        acc[1] += mixed[:, T:] + nn(
            jnp.concatenate([w1, w1], axis=1), jnp.concatenate([dh, dl], axis=0)
        )

    def prepare():
        for i in range(4, 7):
            arrived(i)
        scale = T ** (-0.5)
        qh, ql = split(scale * (wide(qo.at[0, 0]) + wide(qo.at[0, 1])))
        ah, al = split(-scale * (wide(qo.at[1, 0]) + wide(qo.at[1, 1])))
        for i, value in enumerate((qh, qh, ql, ah, ah, al)):
            qa[:, i * T : (i + 1) * T] = value
        acc[0] = wide(qo.at[2, 0])
        acc[1] = wide(qo.at[2, 1])
        for i in range(7, 10):
            arrived(i)

    def turn():
        weights_in.wait()

        @pl.loop(0, 20)
        def _(i):
            cols = pl.ds(pl.multiple_of(i * T, T), T)
            wt[cols, :] = wt_in[:, cols].T

    def needed(entry):
        kind, rest = entry[0], entry[1:]
        if kind in ("y", "x"):
            chunk, away = rest
            if away == 2:
                receive(kind, chunk, -CHUNKS[chunk][3])
            deliver(entry, chunk, kind == "y", (0, 1), away)
        elif kind in ("yx", "xy"):
            chunk, group, away = rest
            if away == 2:
                receive(kind, chunk, group, -CHUNKS[chunk][3])
            else:
                for first in {"all": (1, -1, 2), "own": (), "rest": (1, -1, 2)}.get(group, (group,) if group else ()):
                    receive(kind[0], chunk, first)
            deliver(entry, chunk, kind == "xy", GROUPS[group] if kind == "xy" else (group, 1), away)
        elif kind == "turn":
            turn()
        elif kind == "query":
            prepare()
        else:
            dy, dx = rest
            for chunk, (_, _, y_first, _) in enumerate(CHUNKS):
                first, second = (dy, dx) if y_first else (dx, dy)
                if second:
                    group = first if y_first else SPLIT[first]
                    receive("yx" if y_first else "xy", chunk, group, second)
                elif first:
                    receive("y" if y_first else "x", chunk, first)
            attend(dy, dx)

    for position, entry in enumerate(ORDER):
        needed(entry)
        if position == 9:
            others_in()
        if position == len(ORDER) // 2:
            pl.semaphore_wait(round_1, 2)
            tell(round_2, along_z[2])
            tell(round_2, along_z[NZ - 2])
        if position == len(ORDER) * 9 // 10:
            pl.semaphore_wait(round_2, 2)

    swap = pltpu.make_async_remote_copy(
        src_ref=acc.at[1 - party],
        dst_ref=outs.at[party],
        send_sem=h_send,
        recv_sem=h_recv,
        device_id=sib,
        device_id_type=pl.DeviceIdType.MESH,
    )
    swap.start()
    outs[party] = acc[party]
    swap.wait_recv()
    oh, ol = split(jnp.concatenate([outs[0], outs[1]], axis=1))
    ohl = jnp.concatenate([oh, ol], axis=1)

    def project(dz, column):
        target = zs[dz] + column
        part = wt[pl.ds(pl.multiple_of(target * COLS, COLS), COLS), :]
        return nt(jnp.concatenate([part, part], axis=1), ohl)

    out_sends = []

    def pass_on(value, i, src, dst, sends_sem, recvs_sem, peer):
        scale = scale_of(value)
        src[i, :COLS] = encode(value, scale)
        src[i, COLS:] = jnp.broadcast_to(scale, (16, T)).astype(BF16)
        out_sends.append(
            pltpu.make_async_remote_copy(
                src_ref=src.at[i],
                dst_ref=dst.at[i],
                send_sem=sends_sem.at[i],
                recv_sem=recvs_sem.at[i],
                device_id=peer,
                device_id_type=pl.DeviceIdType.MESH,
            )
        )
        out_sends[-1].start()
        return out_sends[-1]

    def incoming(ref, i):
        return decode(ref[i, :COLS], ref[i, COLS:][:1].astype(F32))

    from_pair = [
        pass_on(project(dz, 1 - ylo), i, ty, ry, y_send, y_recv, pair) for i, dz in enumerate(STEPS)
    ]
    for one in swaps + sends + [swap]:
        one.wait_send()
    from_z = []
    for i, dz in enumerate(STEPS):
        value = project(dz, ylo)
        from_pair[i].wait_recv()
        value += incoming(ry, i)
        if dz:
            from_z.append(pass_on(value, i, tz, rz, z_send, z_recv, along_z[dz]))
    for i, one in enumerate(from_z):
        one.wait_recv()
        value += incoming(rz, i)
    out_ref[...] = value
    for one in out_sends:
        one.wait_send()


def body(
    query_share, key_share, value_share, query_mask, key_mask, value_mask,
    score_triple, square_triple, weight_mask, output_triple, out_weight,
):
    dma = pltpu.SemaphoreType.DMA
    result = pl.pallas_call(
        kernel,
        out_shape=jax.ShapeDtypeStruct((COLS, T), F32),
        in_specs=[pl.BlockSpec(memory_space=pl.ANY)] * 11,
        out_specs=pl.BlockSpec(memory_space=pltpu.VMEM),
        scratch_shapes=[
            pltpu.VMEM((4, 2, T, T), BF16),
            pltpu.VMEM((3, 2, T, T), BF16),
            pltpu.VMEM((3, 2, T, SLOTS * T), BF16),
            pltpu.VMEM((2 * T, 16 * COLS), BF16),
            pltpu.VMEM((16 * COLS, 2 * T), BF16),
            pltpu.VMEM((NY, NX, BLOCK, T), BF16),
            pltpu.VMEM((T, 6 * T), BF16),
            pltpu.VMEM((2, T, T), F32),
            pltpu.VMEM((2, T, T), F32),
            pltpu.VMEM((NZ, COLS + 16, T), BF16),
            pltpu.VMEM((NZ, COLS + 16, T), BF16),
            pltpu.VMEM((NZ - 1, COLS + 16, T), BF16),
            pltpu.VMEM((NZ - 1, COLS + 16, T), BF16),
            dma((10,)),
            dma((10,)),
            dma((10,)),
            dma,
            dma((MESSAGES,)),
            dma((MESSAGES,)),
            dma,
            dma,
            dma((NZ,)),
            dma((NZ,)),
            dma((NZ - 1,)),
            dma((NZ - 1,)),
            pltpu.SemaphoreType.REGULAR,
            pltpu.SemaphoreType.REGULAR,
        ],
        compiler_params=pltpu.CompilerParams(
            collective_id=0, has_side_effects=True, vmem_limit_bytes=60 * 1024 * 1024
        ),
    )(
        key_share, key_mask, value_share, value_mask, query_share, query_mask, output_triple,
        score_triple, square_triple, weight_mask, out_weight,
    )
    return result.T[None]


def solution(mesh):
    shares = P("party", "head", "seq", None)
    return jax.shard_map(
        body,
        mesh=mesh,
        in_specs=(shares,) * 10 + (P("head", None),),
        out_specs=P("party", "seq", "head"),
        check_vma=False,
    )
```

```python
import functools

import jax
import jax.numpy as jnp
from jax import lax
from jax.experimental import pallas as pl
from jax.experimental.pallas import tpu as pltpu
from jax.sharding import PartitionSpec as P

F32 = jnp.float32
BF16 = jnp.bfloat16
T = 128
NX, NY, NZ = 4, 4, 8
SLOTS = NX * NY
REL = {0: 0, -1: 1, 1: 2, 2: 3, -2: 3}
COLS = 160
K, B, SCALES, D, C0, C1 = 0, T, 2 * T, 2 * T + 16, 3 * T + 16, 4 * T + 16
BLOCK = 5 * T + 16
CHUNKS = ((0, 272, True, 1), (272, 272, True, -1), (544, 64, False, 1), (608, 48, False, -1))
ORDER = (
    ("y", 0, -1),
    ("y", 1, 1),
    ("x", 3, 1),
    ("yx", 0, 0, -1),
    ("yx", 1, 0, 1),
    ("x", 2, 1),
    ("x", 3, -1),
    ("x", 2, -1),
    ("x", 3, 2),
    ("y", 1, -1),
    ("yx", 1, 0, -1),
    ("yx", 0, 0, 1),
    ("y", 0, 1),
    ("yx", 0, 0, 2),
    ("x", 2, 2),
    ("yx", 1, 0, 2),
    ("y", 1, 2),
    ("yx", 0, -1, 1),
    ("y", 0, 2),
    ("yx", 1, 1, -1),
    ("yx", 1, 1, 1),
    ("yx", 0, -1, -1),
    ("turn",),
    ("yx", 1, -1, 1),
    ("xy", 3, "rest", 1),
    ("yx", 0, 1, -1),
    ("xy", 2, "own", -1),
    ("xy", 2, "rest", -1),
    ("query",),
    ("yx", 0, 1, 1),
    ("yx", 1, -1, -1),
    ("xy", 3, "own", 1),
    ("attend", 0, 1),
    ("xy", 2, "rest", 1),
    ("yx", 1, 1, 2),
    ("yx", 0, 2, -1),
    ("xy", 3, "own", -1),
    ("attend", 0, -1),
    ("xy", 3, "rest", -1),
    ("attend", 0, 2),
    ("yx", 0, 1, 2),
    ("yx", 1, 2, 1),
    ("attend", 0, 0),
    ("xy", 2, "own", 1),
    ("yx", 1, 2, -1),
    ("xy", 2, "own", 2),
    ("xy", 3, "own", 2),
    ("yx", 1, -1, 2),
    ("xy", 2, "rest", 2),
    ("xy", 3, "rest", 2),
    ("yx", 0, -1, 2),
    ("attend", -1, 0),
    ("yx", 0, 2, 1),
    ("attend", 1, -1),
    ("yx", 0, 2, 2),
    ("attend", 1, 1),
    ("attend", -1, -1),
    ("yx", 1, 2, 2),
    ("attend", 2, 0),
    ("attend", 1, 2),
    ("attend", -1, 1),
    ("attend", 1, 0),
    ("attend", 2, 1),
    ("attend", 2, -1),
    ("attend", -1, 2),
    ("attend", 2, 2),
)
GROUPS = {"all": (0, 4), "own": (0, 1), "rest": (1, 3)}
SPLIT = {0: "own", 1: "rest", -1: "rest", 2: "rest"}
MESSAGES = sum(entry[0] in ("y", "x", "yx", "xy") for entry in ORDER)
POWER = 16
STEPS = (4, 3, 5, 2, 6, 1, 7, 0)
TOP = 2.0 ** (126 / POWER)


def split(value):
    high = value.astype(BF16)
    return high, (value - high.astype(F32)).astype(BF16)


def scale_of(value):
    top = jnp.maximum(jnp.max(jnp.abs(value), axis=0, keepdims=True), 1e-30)
    return (top * 1.01).astype(BF16).astype(F32)


def encode(value, scale):
    code = jnp.abs(value) * (TOP / scale)
    for _ in range(4):
        code = code * code
    return jnp.where(value < 0, -code, code).astype(BF16)


def decode(code, scale):
    code = code.astype(F32)
    size = jnp.exp2(jnp.log2(jnp.maximum(jnp.abs(code), 2.0**-126)) * (1 / POWER)) * (scale / TOP)
    return jnp.where(code < 0, -size, size)


def nt(left, right):
    return lax.dot_general(left, right, (((1,), (1,)), ((), ())), preferred_element_type=F32)


def nn(left, right):
    return lax.dot_general(left, right, (((1,), (0,)), ((), ())), preferred_element_type=F32)


def kernel(
    ks, km, vs, vm, qs, qm, ot, zt, st, wm, ow, out_ref,
    kv, qo, big, wt_in, wt, gat, qa, acc, outs, ty, ry, tz, rz,
    loc_sem, swp_send, swp_recv, w_sem, g_send, g_recv, h_send, h_recv, y_send, y_recv, z_send, z_recv, round_1, round_2,
):
    party = lax.axis_index("party")
    head = lax.axis_index("head")
    seq = lax.axis_index("seq")
    z, ylo = head // 2, head % 2
    yh, x = seq // NX, seq % NX
    xs = {step: lax.rem(x + step + NX, NX) for step in (0, 1, -1, 2)}
    ys = {step: lax.rem(yh + step + NY, NY) for step in (0, 1, -1, 2)}
    zs = {step: lax.rem(z + step, NZ) * 2 for step in range(NZ)}
    sib = (1 - party, head, seq)
    pair = (party, z * 2 + 1 - ylo, seq)
    along_x = {step: (party, head, yh * NX + xs[step]) for step in (1, -1)}
    along_y = {step: (party, head, ys[step] * NX + x) for step in (1, -1)}
    along_z = {step: (party, zs[step] + ylo, seq) for step in range(1, NZ)}
    peers = [
        sib, along_x[1], along_x[-1], along_y[1], along_y[-1], along_z[1], along_z[NZ - 1], pair
    ]

    def tell(semaphore, peer):
        pl.semaphore_signal(semaphore, inc=1, device_id=peer, device_id_type=pl.DeviceIdType.MESH)

    barrier = pltpu.get_barrier_semaphore()
    for peer in peers:
        tell(barrier, peer)

    arrays = [ks, km, vs, vm, qs, qm, ot, zt, st, wm]
    places = [kv.at[i] for i in range(4)] + [qo.at[i] for i in range(3)] + [big.at[i] for i in range(3)]
    locals_ = [
        pltpu.make_async_copy(src.at[0, party], dst.at[party], loc_sem.at[i])
        for i, (src, dst) in enumerate(zip(arrays, places))
    ]
    swaps = [
        pltpu.make_async_remote_copy(
            src_ref=src.at[0, 1 - party],
            dst_ref=dst.at[party],
            send_sem=swp_send.at[i],
            recv_sem=swp_recv.at[i],
            device_id=sib,
            device_id_type=pl.DeviceIdType.MESH,
        )
        for i, (src, dst) in enumerate(zip(arrays, places))
    ]
    weights_in = pltpu.make_async_copy(ow, wt_in, w_sem)
    for one in locals_[:4]:
        one.start()
    pl.semaphore_wait(barrier, len(peers))
    for one in swaps[:4]:
        one.start()

    tell(round_1, along_z[1])
    tell(round_1, along_z[NZ - 1])

    def arrived(i):
        locals_[i].wait()
        swaps[i].wait_recv()

    def wide(ref):
        return ref[...].astype(F32)

    sends = []
    copies = {}

    def message(key, chunk, y_axis, step, y_blocks, x_blocks):
        start, count = CHUNKS[chunk][:2]
        (y0, ny), (x0, nx) = y_blocks, x_blocks
        src = gat.at[pl.ds(REL[y0] if ny == 1 else y0, ny), pl.ds(REL[x0] if nx == 1 else x0, nx), pl.ds(start, count)]
        if y_axis:
            y0 = y0 - step
        else:
            x0 = x0 - step
        dst = gat.at[pl.ds(REL[y0] if ny == 1 else y0, ny), pl.ds(REL[x0] if nx == 1 else x0, nx), pl.ds(start, count)]
        index = len(copies)
        copies[key] = pltpu.make_async_remote_copy(
            src_ref=src,
            dst_ref=dst,
            send_sem=g_send.at[index],
            recv_sem=g_recv.at[index],
            device_id=along_y[step] if y_axis else along_x[step],
            device_id_type=pl.DeviceIdType.MESH,
        )
        copies[key].start()
        sends.append(copies[key])

    def deliver(key, chunk, y_axis, others, away):
        sign = CHUNKS[chunk][3]
        step = -sign if away == sign else sign
        block = (-sign if away == 2 else 0, 1)
        message(key, chunk, y_axis, step, *((block, others) if y_axis else (others, block)))

    received = set()

    def receive(*key):
        if key in received:
            return
        received.add(key)
        copies[key].wait_recv()

    scales = []

    def place(i, value):
        scales.append(scale_of(value))
        gat[0, 0, i : i + T] = encode(value, scales[-1])

    for i in range(4):
        arrived(i)
    place(K, wide(kv.at[0, 0]) + wide(kv.at[0, 1]))
    place(B, wide(kv.at[1, 0]) + wide(kv.at[1, 1]))
    place(D, (wide(kv.at[2, 0]) - wide(kv.at[3, 0])) + (wide(kv.at[2, 1]) - wide(kv.at[3, 1])))
    row = lax.broadcasted_iota(jnp.int32, (16, T), 0)
    gat[0, 0, SCALES:D] = jnp.where(row == 0, scales[0], jnp.where(row == 1, scales[1], scales[2])).astype(BF16)
    gat[0, 0, C0:C1] = kv[3, 0]
    gat[0, 0, C1:] = kv[3, 1]

    def others_in():
        weights_in.start()
        for one in locals_[4:] + swaps[4:]:
            one.start()

    def attend(dy, dx):
        slot = ys[dy] * NX + xs[dx]
        ry, rx = REL[dy], REL[dx]
        cols = pl.ds(pl.multiple_of(slot * T, T), T)
        scales = gat[ry, rx, SCALES:D].astype(F32)
        (kh, kl), (bh, bl), (dh, dl) = [
            split(decode(gat[ry, rx, start : start + T], scales[i : i + 1]))
            for i, start in enumerate((K, B, D))
        ]
        c0 = gat[ry, rx, C0:C1]
        c1 = gat[ry, rx, C1:]
        scores = nt(qa[...], jnp.concatenate([kh, kl, kh, bh, bl, bh], axis=1))
        zz = big[0, 0, :, cols].astype(F32) + big[0, 1, :, cols].astype(F32)
        sq = big[1, 0, :, cols].astype(F32) + big[1, 1, :, cols].astype(F32)
        w0 = big[2, 0, :, cols]
        w1 = big[2, 1, :, cols]
        poly = 1.25 + zz + 0.25 * sq + scores * (1.0 + 0.5 * zz + 0.25 * scores)
        row = seq * T + lax.broadcasted_iota(jnp.int32, (T, T), 0)
        col = slot * T + lax.broadcasted_iota(jnp.int32, (T, T), 1)
        weights = jnp.where(col <= row, poly * lax.rsqrt((row + 1).astype(F32)), 0.0)
        lead = weights - w1.astype(F32)
        opened = lead - w0.astype(F32)
        lh, ll = split(lead)
        oh, ol = split(opened)
        both = jnp.concatenate([c0, c1], axis=1)
        mixed = nn(jnp.concatenate([oh, ol], axis=1), jnp.concatenate([both, both], axis=0))
        acc[0] += mixed[:, :T] + nn(
            jnp.concatenate([lh, ll, lh], axis=1), jnp.concatenate([dh, dh, dl], axis=0)
        )
        acc[1] += mixed[:, T:] + nn(
            jnp.concatenate([w1, w1], axis=1), jnp.concatenate([dh, dl], axis=0)
        )

    def prepare():
        for i in range(4, 7):
            arrived(i)
        scale = T ** (-0.5)
        qh, ql = split(scale * (wide(qo.at[0, 0]) + wide(qo.at[0, 1])))
        ah, al = split(-scale * (wide(qo.at[1, 0]) + wide(qo.at[1, 1])))
        for i, value in enumerate((qh, qh, ql, ah, ah, al)):
            qa[:, i * T : (i + 1) * T] = value
        acc[0] = wide(qo.at[2, 0])
        acc[1] = wide(qo.at[2, 1])
        for i in range(7, 10):
            arrived(i)

    def turn():
        weights_in.wait()

        @pl.loop(0, 20)
        def _(i):
            cols = pl.ds(pl.multiple_of(i * T, T), T)
            wt[cols, :] = wt_in[:, cols].T

    def needed(entry):
        kind, rest = entry[0], entry[1:]
        if kind in ("y", "x"):
            chunk, away = rest
            if away == 2:
                receive(kind, chunk, -CHUNKS[chunk][3])
            deliver(entry, chunk, kind == "y", (0, 1), away)
        elif kind in ("yx", "xy"):
            chunk, group, away = rest
            if away == 2:
                receive(kind, chunk, group, -CHUNKS[chunk][3])
            else:
                for first in {"all": (1, -1, 2), "own": (), "rest": (1, -1, 2)}.get(group, (group,) if group else ()):
                    receive(kind[0], chunk, first)
            deliver(entry, chunk, kind == "xy", GROUPS[group] if kind == "xy" else (group, 1), away)
        elif kind == "turn":
            turn()
        elif kind == "query":
            prepare()
        else:
            dy, dx = rest
            for chunk, (_, _, y_first, _) in enumerate(CHUNKS):
                first, second = (dy, dx) if y_first else (dx, dy)
                if second:
                    group = first if y_first else SPLIT[first]
                    receive("yx" if y_first else "xy", chunk, group, second)
                elif first:
                    receive("y" if y_first else "x", chunk, first)
            attend(dy, dx)

    for position, entry in enumerate(ORDER):
        needed(entry)
        if position == 9:
            others_in()
        if position == len(ORDER) // 2:
            pl.semaphore_wait(round_1, 2)
            tell(round_2, along_z[2])
            tell(round_2, along_z[NZ - 2])
        if position == len(ORDER) * 9 // 10:
            pl.semaphore_wait(round_2, 2)

    swap = pltpu.make_async_remote_copy(
        src_ref=acc.at[1 - party],
        dst_ref=outs.at[party],
        send_sem=h_send,
        recv_sem=h_recv,
        device_id=sib,
        device_id_type=pl.DeviceIdType.MESH,
    )
    swap.start()
    outs[party] = acc[party]
    swap.wait_recv()
    oh, ol = split(jnp.concatenate([outs[0], outs[1]], axis=1))
    ohl = jnp.concatenate([oh, ol], axis=0)

    def project(dz, column):
        target = zs[dz] + column
        part = wt[pl.ds(pl.multiple_of(target * COLS, COLS), COLS), :]
        both = nt(part, ohl)
        return both[:, :T] + both[:, T:]

    out_sends = []

    def pass_on(value, i, src, dst, sends_sem, recvs_sem, peer):
        scale = scale_of(value)
        src[i, :COLS] = encode(value, scale)
        src[i, COLS:] = jnp.broadcast_to(scale, (16, T)).astype(BF16)
        out_sends.append(
            pltpu.make_async_remote_copy(
                src_ref=src.at[i],
                dst_ref=dst.at[i],
                send_sem=sends_sem.at[i],
                recv_sem=recvs_sem.at[i],
                device_id=peer,
                device_id_type=pl.DeviceIdType.MESH,
            )
        )
        out_sends[-1].start()
        return out_sends[-1]

    def incoming(ref, i):
        return decode(ref[i, :COLS], ref[i, COLS:][:1].astype(F32))

    from_pair = [
        pass_on(project(dz, 1 - ylo), i, ty, ry, y_send, y_recv, pair) for i, dz in enumerate(STEPS)
    ]
    from_z = []
    for i, dz in enumerate(STEPS):
        value = project(dz, ylo)
        from_pair[i].wait_recv()
        value += incoming(ry, i)
        if dz:
            from_z.append(pass_on(value, i, tz, rz, z_send, z_recv, along_z[dz]))
    for one in swaps + sends + [swap]:
        one.wait_send()
    for i, one in enumerate(from_z):
        one.wait_recv()
        value += incoming(rz, i)
    out_ref[...] = value
    for one in out_sends:
        one.wait_send()


def body(
    query_share, key_share, value_share, query_mask, key_mask, value_mask,
    score_triple, square_triple, weight_mask, output_triple, out_weight,
):
    dma = pltpu.SemaphoreType.DMA
    result = pl.pallas_call(
        kernel,
        out_shape=jax.ShapeDtypeStruct((COLS, T), F32),
        in_specs=[pl.BlockSpec(memory_space=pl.ANY)] * 11,
        out_specs=pl.BlockSpec(memory_space=pltpu.VMEM),
        scratch_shapes=[
            pltpu.VMEM((4, 2, T, T), BF16),
            pltpu.VMEM((3, 2, T, T), BF16),
            pltpu.VMEM((3, 2, T, SLOTS * T), BF16),
            pltpu.VMEM((2 * T, 16 * COLS), BF16),
            pltpu.VMEM((16 * COLS, 2 * T), BF16),
            pltpu.VMEM((NY, NX, BLOCK, T), BF16),
            pltpu.VMEM((T, 6 * T), BF16),
            pltpu.VMEM((2, T, T), F32),
            pltpu.VMEM((2, T, T), F32),
            pltpu.VMEM((NZ, COLS + 16, T), BF16),
            pltpu.VMEM((NZ, COLS + 16, T), BF16),
            pltpu.VMEM((NZ - 1, COLS + 16, T), BF16),
            pltpu.VMEM((NZ - 1, COLS + 16, T), BF16),
            dma((10,)),
            dma((10,)),
            dma((10,)),
            dma,
            dma((MESSAGES,)),
            dma((MESSAGES,)),
            dma,
            dma,
            dma((NZ,)),
            dma((NZ,)),
            dma((NZ - 1,)),
            dma((NZ - 1,)),
            pltpu.SemaphoreType.REGULAR,
            pltpu.SemaphoreType.REGULAR,
        ],
        compiler_params=pltpu.CompilerParams(
            collective_id=0, has_side_effects=True, vmem_limit_bytes=60 * 1024 * 1024
        ),
    )(
        key_share, key_mask, value_share, value_mask, query_share, query_mask, output_triple,
        score_triple, square_triple, weight_mask, out_weight,
    )
    return result.T[None]


def solution(mesh):
    shares = P("party", "head", "seq", None)
    return jax.shard_map(
        body,
        mesh=mesh,
        in_specs=(shares,) * 10 + (P("head", None),),
        out_specs=P("party", "seq", "head"),
        check_vma=False,
    )
```
